32 devices in a mesh: occ: 4 (over x, core), virt: 8 (over z, y).
Axes of the slice: x: 2, y: 2, z: 4, core: 2. Of those that a mesh axis runs over, the one named last changes fastest.
Arguments:
- integrals: bfloat16 [48, 1024, 2048], P('occ', 'virt'), may hold values from -1 to 1
- occ_energy: float32 [48], replicated, may hold values from -2 to -0.5
- virt_energy: float32 [1024], replicated, may hold values from 0.2 to 3
- partners: int32 [2], replicated, may hold values from 0 to 47
Outputs:
- gamma: bfloat16 [48, 1024, 2048], P('occ', 'virt')
The draws below stay inside these ranges and needn't reach their ends.
All inputs are finite; a program needn't handle non-finite values.
Results may differ from the reference program's by a relative error of at most 0.0043.
Values may be sent and summed in bfloat16 or wider, within the bound.
No kernel may reach another device: no remote copies, remote signals or barrier semaphores. Data moves between devices by JAX's collectives and lax.ppermute only.
A program may use at most 64 MiB of HBM per device.

```python
import jax
import jax.numpy as jnp
from jax import lax

NV = 1024
NAUX = 2048
STEPS = 2
NOCC = 48


def steps_of(key, shape, shards, least, largest):
    def one(position, blocks):
        draws = jax.random.uniform(jax.random.fold_in(jax.random.fold_in(key, 6), position), (blocks,), jnp.float32, least / len(shards), largest / len(shards))
        return jnp.repeat(jnp.exp(draws), shape[position] // blocks).reshape((-1,) + (1,) * (len(shape) - position - 1))

    factor_of = one(*shards[0])
    for cut in shards[1:]:
        factor_of = factor_of * one(*cut)
    return factor_of


def gaussian(rng, shape, width, reach, split=(), dtype=jnp.bfloat16):
    array = width * jax.random.normal(rng, shape, jnp.float32)
    if split:
        array = array * steps_of(rng, shape, split, -0.22, 0.18)
    return jnp.clip(array, -reach, reach).astype(dtype)


def setup_inputs(seed: int = 0) -> dict:
    keys = jax.random.split(jax.random.key(seed), 5)
    integrals = gaussian(keys[0], (NOCC, NV, NAUX), 0.125, 1.0, ((0, 4), (1, 8)))
    occ_energy = jnp.clip(jax.random.uniform(keys[1], (NOCC,), jnp.float32, -2.0, -0.5), -2.0, -0.5)
    virt_energy = jnp.clip(jax.random.uniform(keys[2], (NV,), jnp.float32, 0.2, 3.0), 0.2, 3.0)
    partners = jax.random.randint(keys[3], (STEPS,), 0, NOCC).astype(jnp.int32)
    return dict(integrals=integrals, occ_energy=occ_energy, virt_energy=virt_energy, partners=partners)


def reference(integrals, occ_energy, virt_energy, partners):
    def one_orbital(inputs):
        occ_block, own_energy = inputs
        total_sum = jnp.zeros(occ_block.shape, jnp.float32)
        for step_index in range(STEPS):
            partner = partners[step_index]
            partner_block = lax.dynamic_index_in_dim(integrals, partner, 0, keepdims=False)
            pair_energy = lax.dynamic_index_in_dim(occ_energy, partner, 0, keepdims=False)
            scores = lax.dot_general(occ_block, partner_block, (((1,), (1,)), ((), ())), preferred_element_type=jnp.float32)
            denominator = virt_energy[:, None] + virt_energy[None, :] - own_energy - pair_energy
            amplitudes = (scores / denominator).astype(jnp.bfloat16)
            total_sum = total_sum + jnp.dot(amplitudes, partner_block, preferred_element_type=jnp.float32)
        return total_sum.astype(jnp.bfloat16)

    return lax.map(one_orbital, (integrals, occ_energy))
```

```python
import jax
import jax.numpy as jnp
from jax import lax
from jax.experimental import pallas as pl
from jax.experimental.pallas import tpu as pltpu
from jax.sharding import PartitionSpec as P

TILE = 256


def contract(rows, blocks, row_energy, block_energy, total, out_dtype):
    height, width = rows.shape
    count, depth = len(blocks), blocks[0].shape[0]
    tile = min(TILE, height)
    while height % tile:
        tile //= 2

    def kernel(rows_ref, row_energy_ref, block_energy_ref, *rest):
        block_refs, rest = rest[:count], rest[count:]
        total_ref = rest[0] if total is not None else None
        out_ref, held, sems = rest[-3:]

        @pl.when(pl.program_id(0) == 0)
        def _():
            copies = [
                pltpu.make_async_copy(block_refs[k], held.at[pl.ds(k * depth, depth)], sems.at[k])
                for k in range(count)
            ]
            for copy in copies:
                copy.start()
            for copy in copies:
                copy.wait()

        scores = lax.dot_general(
            rows_ref[...], held[...], (((1,), (1,)), ((), ())), preferred_element_type=jnp.float32
        )
        amplitudes = (scores / (row_energy_ref[...] + block_energy_ref[...])).astype(jnp.bfloat16)
        result = jnp.dot(amplitudes, held[...], preferred_element_type=jnp.float32)
        if total_ref is not None:
            result = result + total_ref[...].astype(jnp.float32)
        out_ref[...] = result.astype(out_dtype)

    row_spec = pl.BlockSpec((tile, width), lambda i: (i, 0))
    specs = [row_spec, pl.BlockSpec((tile, 1), lambda i: (i, 0)), pl.BlockSpec((1, count * depth), lambda i: (0, 0))]
    specs += [pl.BlockSpec(memory_space=pl.ANY)] * count
    operands = [rows, row_energy, block_energy, *blocks]
    if total is not None:
        specs.append(row_spec)
        operands.append(total)
    return pl.pallas_call(
        kernel,
        grid=(height // tile,),
        in_specs=specs,
        out_specs=row_spec,
        out_shape=jax.ShapeDtypeStruct((height, width), out_dtype),
        scratch_shapes=[pltpu.VMEM((count * depth, width), jnp.bfloat16), pltpu.SemaphoreType.DMA((count,))],
        compiler_params=pltpu.CompilerParams(vmem_limit_bytes=48 << 20),
        cost_estimate=pl.CostEstimate(
            flops=4 * height * width * count * depth,
            bytes_accessed=2 * height * width * 2 + 2 * count * depth * width,
            transcendentals=0,
        ),
    )(*operands)


def per_device(occ_size, virt_size, integrals, occ_energy, virt_energy, partners):
    occ_dev, local_virt, aux_width = integrals.shape
    occ_index, virt_index = lax.axis_index("occ"), lax.axis_index("virt")
    core = occ_index % 2
    ring = virt_size // 2

    def swap_occ(value, bit):
        return lax.ppermute(value, "occ", [(o, o ^ bit) for o in range(occ_size)])

    def swap_pair(value):
        return lax.ppermute(value, "virt", [(v, v ^ 1) for v in range(virt_size)])

    def shift_ring(value):
        return lax.ppermute(value, "virt", [(v, (v + 2) % virt_size) for v in range(virt_size)])

    def kept(step):
        partner = partners[step]
        row = lax.dynamic_index_in_dim(integrals, partner % occ_dev, 0, keepdims=False)
        return jnp.where(partner // occ_dev == occ_index, row, 0).astype(row.dtype)

    def held_by(step, bits):
        return (partners[step] // occ_dev) & ~bits == occ_index & ~bits

    mine, other = core, 1 - core
    own = kept(mine)
    got = swap_occ(kept(other), 1)
    own = jnp.where(partners[mine] // occ_dev == occ_index, own, got)
    bit = 2
    while bit < occ_size:
        got = swap_occ(own, bit)
        own = jnp.where(held_by(mine, bit - 1), own, got)
        bit *= 2

    straight = [own]
    for _ in range(ring - 1):
        straight.append(shift_ring(straight[-1]))
    crossed = [swap_pair(block) for block in straight]

    own_energy = lax.dynamic_slice_in_dim(occ_energy, occ_index * occ_dev, occ_dev)
    local_energy = lax.dynamic_slice_in_dim(virt_energy, virt_index * local_virt, local_virt)
    row_energy = (local_energy[None, :] - own_energy[:, None]).reshape(-1, 1)

    def energy_of(step, position):
        values = lax.dynamic_slice_in_dim(virt_energy, position * local_virt, local_virt)
        return values - occ_energy[partners[step]]

    def pieces(block, position):
        return [(block, energy_of(mine, position)), (swap_occ(block, 1), energy_of(other, position))]

    rows = integrals.reshape(occ_dev * local_virt, aux_width)
    positions = [(virt_index - 2 * k) % virt_size for k in range(ring)]
    arrivals = []
    for k in range(ring):
        arrivals.append(pieces(straight[k], positions[k]))
        arrivals.append(pieces(crossed[k], positions[k] ^ 1))

    groups, total = group_arrivals(arrivals), None
    for index, group in enumerate(groups):
        last = index == len(groups) - 1
        total = contract(
            rows,
            [block for block, _ in group],
            row_energy,
            jnp.concatenate([energy for _, energy in group])[None, :],
            total,
            jnp.bfloat16 if last else jnp.float32,
        )
    return total.reshape(integrals.shape)


def group_arrivals(arrivals):
    count = len(arrivals)
    cuts = [0, 3 * count // 8, 5 * count // 8, 7 * count // 8, count]
    return [sum(arrivals[a:b], []) for a, b in zip(cuts, cuts[1:]) if b > a]


def solution(mesh):
    in_specs = (P("occ", "virt", None), P(), P(), P())
    out_specs = P("occ", "virt", None)

    def run(integrals, occ_energy, virt_energy, partners):
        return per_device(
            mesh.shape["occ"], mesh.shape["virt"], integrals, occ_energy, virt_energy, partners
        )

    return jax.shard_map(run, mesh=mesh, in_specs=in_specs, out_specs=out_specs, check_vma=False)
```

```python
import jax
import jax.numpy as jnp
from jax import lax
from jax.experimental import pallas as pl
from jax.experimental.pallas import tpu as pltpu
from jax.sharding import PartitionSpec as P

VMEM = pl.BlockSpec(memory_space=pltpu.VMEM)
ANY = pl.BlockSpec(memory_space=pl.ANY)


def tile_of(height, largest):
    return max(t for t in range(16, largest + 1, 16) if height % t == 0)


def bring(rows):
    def kernel(rows_ref, out_ref):
        pltpu.sync_copy(rows_ref, out_ref)

    return pl.pallas_call(
        kernel,
        in_specs=[ANY],
        out_specs=VMEM,
        out_shape=pltpu.VMEM(rows.shape, rows.dtype),
        compiler_params=pltpu.CompilerParams(vmem_limit_bytes=8 << 20),
    )(rows)


def contract(rows, blocks, row_energy, block_energy, total, last):
    height, width = rows.shape
    count, depth = len(blocks), blocks[0].shape[0]
    tile = tile_of(height, 512)
    tiles = height // tile

    def kernel(rows_ref, row_energy_ref, block_energy_ref, *rest):
        block_refs, rest = rest[:count], rest[count:]
        total_ref, rest = (rest[0], rest[1:]) if total is not None else (None, rest)
        out_ref, token_ref, held, sems = rest[:4]
        copies = [
            pltpu.make_async_copy(block_refs[k], held.at[pl.ds(k * depth, depth)], sems.at[k]) for k in range(count)
        ]
        for copy in copies:
            copy.start()
        token_ref[...] = jnp.zeros_like(token_ref)
        for copy in copies:
            copy.wait()
        writes = []
        for i in range(tiles):
            at = pl.ds(i * tile, tile)
            scores = lax.dot_general(
                rows_ref[at, :], held[...], (((1,), (1,)), ((), ())), preferred_element_type=jnp.float32
            )
            amplitudes = (scores / (row_energy_ref[at, :] + block_energy_ref[...])).astype(jnp.bfloat16)
            result = jnp.dot(amplitudes, held[...], preferred_element_type=jnp.float32)
            if total_ref is not None:
                result = result + total_ref[at, :]
            if last:
                staged, write_sems = rest[4:]
                if i >= 2:
                    writes[i - 2].wait()
                staged[i % 2] = result.astype(jnp.bfloat16)
                write = pltpu.make_async_copy(staged.at[i % 2], out_ref.at[at, :], write_sems.at[i])
                write.start()
                writes.append(write)
            else:
                out_ref[at, :] = result
        for write in writes[-2:]:
            write.wait()

    operands = [rows, row_energy, block_energy, *blocks]
    specs = [VMEM] * 3 + [ANY] * count
    if total is not None:
        operands.append(total)
        specs.append(VMEM)
    scratch = [pltpu.VMEM((count * depth, width), jnp.bfloat16), pltpu.SemaphoreType.DMA((count,))]
    if last:
        scratch += [pltpu.VMEM((2, tile, width), jnp.bfloat16), pltpu.SemaphoreType.DMA((tiles,))]
        out = jax.ShapeDtypeStruct((height, width), jnp.bfloat16)
    else:
        out = pltpu.VMEM((height, width), jnp.float32)
    return pl.pallas_call(
        kernel,
        in_specs=specs,
        out_specs=(ANY if last else VMEM, VMEM),
        out_shape=(out, jax.ShapeDtypeStruct((8, 128), jnp.float32)),
        scratch_shapes=scratch,
        input_output_aliases={3 + count: 0} if total is not None and not last else {},
        compiler_params=pltpu.CompilerParams(vmem_limit_bytes=16 << 20),
        cost_estimate=pl.CostEstimate(
            flops=4 * height * width * count * depth, bytes_accessed=2 * count * depth * width, transcendentals=0
        ),
    )(*operands)


def gate(tokens, values):
    count, skip = len(values), len(tokens)

    def kernel(*refs):
        del refs

    return pl.pallas_call(
        kernel,
        in_specs=[ANY] * (skip + count),
        out_specs=[ANY] * count,
        out_shape=[jax.ShapeDtypeStruct(value.shape, value.dtype) for value in values],
        input_output_aliases={skip + k: k for k in range(count)},
        compiler_params=pltpu.CompilerParams(vmem_limit_bytes=1 << 20),
    )(*tokens, *values)


def per_device(occ_size, virt_size, integrals, occ_energy, virt_energy, partners):
    occ_dev, local_virt, aux_width = integrals.shape
    occ_index, virt_index = lax.axis_index("occ"), lax.axis_index("virt")
    core, plane = occ_index % 2, occ_index // 2 % 2
    ring, half = virt_size // 2, local_virt // 2

    def swap_occ(value, bit):
        return lax.ppermute(value, "occ", [(o, o ^ bit) for o in range(occ_size)])

    def swap_pair(value):
        return lax.ppermute(value, "virt", [(v, v ^ 1) for v in range(virt_size)])

    def shift_ring(value):
        return lax.ppermute(value, "virt", [(v, (v - 2) % virt_size) for v in range(virt_size)])

    mine, other = partners[core], partners[1 - core]
    owner = mine // occ_dev
    own = lax.dynamic_index_in_dim(integrals, mine % occ_dev, 0, keepdims=False)
    sent = lax.dynamic_index_in_dim(integrals, other % occ_dev, 0, keepdims=False)
    own = jnp.where(owner == occ_index, own, swap_occ(sent, 1))

    def half_of(which):
        return lax.dynamic_slice_in_dim(own, which * half, half)

    halves = [half_of(plane), half_of(1 - plane)]
    bit = 2
    while bit < occ_size:
        sent = halves[::-1] if bit == 2 else halves
        held = owner & ~(bit - 1) == occ_index & ~(bit - 1)
        halves = [jnp.where(held, kept, swap_occ(value, bit)) for kept, value in zip(halves, sent)]
        bit *= 2

    rows = bring(integrals.reshape(occ_dev * local_virt, aux_width))
    own_energy = lax.dynamic_slice_in_dim(occ_energy, occ_index * occ_dev, occ_dev)
    local_energy = lax.dynamic_slice_in_dim(virt_energy, virt_index * local_virt, local_virt)
    row_energy = (local_energy[None, :] - own_energy[:, None]).reshape(-1, 1)
    ringed = lax.dynamic_slice_in_dim(
        jnp.concatenate([virt_energy, virt_energy]), virt_index // 2 * 2 * local_virt, virt_size * local_virt
    ).reshape(ring, 2, 2, half)
    ringed = jnp.where(virt_index % 2 == 0, ringed, ringed[:, ::-1])
    ringed = jnp.where(plane == 0, ringed, ringed[:, :, ::-1])
    pair = jnp.stack([occ_energy[mine], occ_energy[other]])
    block_energy = (ringed[:, :, :, None] - pair[None, None, None, :, None]).reshape(ring * 2, 1, 4 * half)

    def both(blocks):
        return [block for value in blocks for block in (value, swap_occ(value, 1))]

    def energy(first, count):
        return block_energy[first : first + count].reshape(1, -1)

    straight = [*gate([rows, row_energy, block_energy], halves[:1]), halves[1]]
    total, token = contract(rows, both(straight), row_energy, energy(0, 1), None, False)
    shifted, crossed = [], []
    for k in range(1, ring):
        arrived, crossed = [], []
        for block in straight:
            moved = gate([token], [shift_ring(block), swap_pair(block)])
            arrived.append(moved[0])
            crossed.append(moved[1])
        blocks = [*both(crossed), *both(arrived)]
        straight = arrived
        total, token = contract(rows, blocks, row_energy, energy(2 * k - 1, 2), total, False)
    crossed = [swap_pair(straight[0]), shift_ring(crossed[1])]
    crossed = gate([token], crossed)
    total, token = contract(rows, both(crossed), row_energy, energy(2 * ring - 1, 1), total, True)
    return total.reshape(integrals.shape)


def solution(mesh):
    in_specs = (P("occ", "virt", None), P(), P(), P())
    out_specs = P("occ", "virt", None)

    def run(integrals, occ_energy, virt_energy, partners):
        return per_device(
            mesh.shape["occ"], mesh.shape["virt"], integrals, occ_energy, virt_energy, partners
        )

    return jax.shard_map(run, mesh=mesh, in_specs=in_specs, out_specs=out_specs, check_vma=False)
```

```python
import jax
import jax.numpy as jnp
from jax import lax
from jax.experimental import pallas as pl
from jax.experimental.pallas import tpu as pltpu
from jax.sharding import PartitionSpec as P

FIRST, SECOND, WHOLE = range(3)

VMEM = pl.BlockSpec(memory_space=pltpu.VMEM)
SMEM = pl.BlockSpec(memory_space=pltpu.SMEM)
ANY = pl.BlockSpec(memory_space=pl.ANY)
TOKEN = jax.ShapeDtypeStruct((8, 128), jnp.float32)


def call(kernel, operands, in_specs, outs, scratch=(), aliases=None, vmem=2):
    return pl.pallas_call(
        kernel,
        in_specs=in_specs,
        out_specs=[spec for spec, _ in outs],
        out_shape=[shape for _, shape in outs],
        scratch_shapes=list(scratch),
        input_output_aliases=aliases or {},
        compiler_params=pltpu.CompilerParams(vmem_limit_bytes=vmem << 20),
        cost_estimate=pl.CostEstimate(flops=0, bytes_accessed=0, transcendentals=0),
    )(*operands)


def extract(partners, integrals):
    occ_dev = integrals.shape[0]
    shape = pltpu.VMEM(integrals.shape[1:], integrals.dtype)

    def kernel(partners_ref, integrals_ref, own_ref, sent_ref, sems):
        core = lax.rem(lax.axis_index("occ"), 2)
        copies = []
        for k, (out_ref, step) in enumerate(((sent_ref, 1 - core), (own_ref, core))):
            row = lax.rem(partners_ref[step], occ_dev)
            copies.append(pltpu.make_async_copy(integrals_ref.at[row], out_ref, sems.at[k]))
        for copy in copies:
            copy.start()
        for copy in copies:
            copy.wait()

    return call(
        kernel,
        [partners, integrals],
        [SMEM, ANY],
        [(VMEM, shape)] * 2,
        [pltpu.SemaphoreType.DMA((2,))],
        vmem=56,
    )


def choose(where, partners, occ_dev, bit, own, got, token=None):
    height, width = own.shape
    half = height // 2
    outs = [(ANY, jax.ShapeDtypeStruct(own.shape, own.dtype))]
    if token is not None:
        outs.append((ANY, jax.ShapeDtypeStruct((half, width), own.dtype)))

    def kernel(where_ref, partners_ref, own_ref, got_ref, *rest):
        out_refs, sems = rest[-1 - len(outs) : -1], rest[-1]
        occ_index = where_ref[1]
        owner = lax.div(partners_ref[lax.rem(occ_index, 2)], occ_dev)
        held = lax.div(owner, bit) == lax.div(occ_index, bit)
        plane = lax.rem(lax.div(occ_index, 2), 2)

        def copy_from(source_ref):
            copies = [pltpu.make_async_copy(source_ref, out_refs[0], sems.at[0])]
            if token is not None:
                source = source_ref.at[pl.ds(pl.multiple_of(plane * half, half), half)]
                copies.append(pltpu.make_async_copy(source, out_refs[1], sems.at[1]))
            for copy in copies:
                copy.start()
            for copy in copies:
                copy.wait()

        pl.when(held)(lambda: copy_from(own_ref))
        pl.when(jnp.logical_not(held))(lambda: copy_from(got_ref))

    operands, specs = [where, partners, own, got], [SMEM, SMEM, ANY, ANY]
    if token is not None:
        operands.append(token)
        specs.append(ANY)
    return call(kernel, operands, specs, outs, [pltpu.SemaphoreType.DMA((2,))], vmem=48 if token is None else 2)


def prepare(where, partners, occ_energy, column, virt_halves, rows, groups, ready):
    height = rows.shape[0]
    local_virt, half = column.shape[0], virt_halves.shape[1]
    occ_dev, virt_size = height // local_virt, virt_halves.shape[0] // 2
    widths = [sum(half * (2 if which == WHOLE else 1) for _, _, which, _ in places) for places in groups]

    def kernel(where_ref, partners_ref, occ_energy_ref, column_ref, virt_ref, rows_ref, *rest):
        rest = rest[1:]
        out_ref, row_energy_ref, token_ref = rest[:3]
        energy_refs, sem = rest[3:-1], rest[-1]
        load = pltpu.make_async_copy(rows_ref, out_ref, sem)
        load.start()
        virt_index, occ_index = where_ref[0], where_ref[1]
        plane = lax.rem(lax.div(occ_index, 2), 2)
        token_ref[...] = jnp.zeros_like(token_ref)
        for i in range(occ_dev):
            own = occ_energy_ref[occ_index * occ_dev + i]
            row_energy_ref[pl.ds(i * local_virt, local_virt), :] = column_ref[...] - own
        for places, energy_ref in zip(groups, energy_refs):
            start = 0
            for ring_step, side, which, step in places:
                position = lax.rem(virt_index + 2 * ring_step, virt_size)
                position = position + side * (1 - 2 * lax.rem(position, 2))
                pair = occ_energy_ref[partners_ref[lax.rem(occ_index + step, 2)]]
                for part in {FIRST: [plane], SECOND: [1 - plane], WHOLE: [0, 1]}[which]:
                    energy_ref[:, start : start + half] = virt_ref[pl.ds(2 * position + part, 1), :] - pair
                    start += half
        load.wait()

    outs = [(VMEM, pltpu.VMEM(rows.shape, rows.dtype)), (VMEM, pltpu.VMEM((height, 1), jnp.float32)), (VMEM, TOKEN)]
    outs += [(VMEM, pltpu.VMEM((1, width), jnp.float32)) for width in widths]
    rows, row_energy, token, *energies = call(
        kernel,
        [where, partners, occ_energy, column, virt_halves, rows, ready],
        [SMEM] * 3 + [VMEM] * 2 + [ANY] * 2,
        outs,
        [pltpu.SemaphoreType.DMA],
        vmem=16,
    )
    return rows, row_energy, token, energies


def contract(rows, row_energy, block_energy, blocks, total, last):
    height, width = rows.shape
    count, depths = len(blocks), [block.shape[0] for block in blocks]
    starts, depth = [sum(depths[:k]) for k in range(count)], sum(depths)
    tile = max(t for t in range(16, 513, 16) if height % t == 0)
    tiles = height // tile

    def kernel(rows_ref, row_energy_ref, block_energy_ref, *rest):
        block_refs, rest = rest[:count], rest[count:]
        total_ref, rest = (rest[0], rest[1:]) if total is not None else (None, rest)
        out_ref, token_ref, held, sems = rest[:4]
        copies = [
            pltpu.make_async_copy(block_refs[k], held.at[pl.ds(starts[k], depths[k])], sems.at[k])
            for k in range(count)
        ]
        for copy in copies:
            copy.start()
        token_ref[...] = jnp.zeros_like(token_ref)
        for copy in copies:
            copy.wait()
        writes = []
        for i in range(tiles):
            at = pl.ds(i * tile, tile)
            scores = lax.dot_general(
                rows_ref[at, :], held[...], (((1,), (1,)), ((), ())), preferred_element_type=jnp.float32
            )
            amplitudes = (scores / (row_energy_ref[at, :] + block_energy_ref[...])).astype(jnp.bfloat16)
            result = jnp.dot(amplitudes, held[...], preferred_element_type=jnp.float32)
            if total_ref is not None:
                result = result + total_ref[at, :]
            if last:
                staged, write_sems = rest[4:]
                if i >= 2:
                    writes[i - 2].wait()
                staged[i % 2] = result.astype(jnp.bfloat16)
                write = pltpu.make_async_copy(staged.at[i % 2], out_ref.at[at, :], write_sems.at[i])
                write.start()
                writes.append(write)
            else:
                out_ref[at, :] = result
        for write in writes[-2:]:
            write.wait()

    operands, specs = [rows, row_energy, block_energy, *blocks], [VMEM] * 3 + [ANY] * count
    if total is not None:
        operands.append(total)
        specs.append(VMEM)
    scratch = [pltpu.VMEM((depth, width), jnp.bfloat16), pltpu.SemaphoreType.DMA((count,))]
    if last:
        scratch += [pltpu.VMEM((2, tile, width), jnp.bfloat16), pltpu.SemaphoreType.DMA((tiles,))]
        out = (ANY, jax.ShapeDtypeStruct((height, width), jnp.bfloat16))
    else:
        out = (VMEM, pltpu.VMEM((height, width), jnp.float32))
    aliases = {3 + count: 0} if total is not None and not last else {}
    return call(kernel, operands, specs, [out, (VMEM, TOKEN)], scratch, aliases, vmem=16)


def gate(tokens, values):
    skip = len(tokens)

    def kernel(*refs):
        del refs

    outs = [(ANY, jax.ShapeDtypeStruct(value.shape, value.dtype)) for value in values]
    aliases = {skip + k: k for k in range(len(values))}
    return call(kernel, [*tokens, *values], [ANY] * (skip + len(values)), outs, aliases=aliases, vmem=1)


def per_device(occ_size, virt_size, integrals, occ_energy, virt_energy, partners):
    occ_dev, local_virt, aux_width = integrals.shape
    occ_index, virt_index = lax.axis_index("occ"), lax.axis_index("virt")
    ring, half = virt_size // 2, local_virt // 2

    def swap_occ(value, bit):
        return lax.ppermute(value, "occ", [(o, o ^ bit) for o in range(occ_size)])

    def swap_pair(value):
        return lax.ppermute(value, "virt", [(v, v ^ 1) for v in range(virt_size)])

    def shift_ring(value, k):
        return lax.ppermute(value, "virt", [(v, (v - 2 * k) % virt_size) for v in range(virt_size)])

    shifts = sorted(range(1, ring), key=lambda k: min(k, ring - k))
    early, late = shifts[: ring // 2], shifts[ring // 2 :]
    even, odd, reach = early[0::2], early[1::2], (len(early) + 1) // 2
    groups = [
        [(0, 0, WHOLE)],
        [(0, 1, WHOLE)] + [(k, 0, FIRST) for k in early],
        [(k, 1, FIRST) for k in even] + [(k, 0, FIRST) for k in late] + [(k, 0, SECOND) for k in early],
        [(k, 0, SECOND) for k in late] + [(k, 1, FIRST) for k in late + odd] + [(k, 1, SECOND) for k in even],
        [(k, 1, SECOND) for k in odd + late],
    ]
    places = [[(*place, step) for place in group for step in range(2)] for group in groups]

    where = jnp.stack([virt_index, occ_index]).astype(jnp.int32)
    column = lax.dynamic_slice_in_dim(virt_energy, virt_index * local_virt, local_virt)[:, None]
    virt_halves = virt_energy.reshape(2 * virt_size, half)
    own, sent = extract(partners, integrals)
    (own,) = choose(where, partners, occ_dev, 1, own, swap_occ(sent, 1))
    rows, row_energy, token, energies = prepare(
        where, partners, occ_energy, column, virt_halves, integrals.reshape(-1, aux_width), places, own
    )
    bit = 2
    while bit < occ_size:
        own, *first_half = choose(where, partners, occ_dev, bit, own, swap_occ(own, bit), token)
        bit *= 2

    blocks = {(0, 0, WHOLE): own, (0, 1, WHOLE): swap_pair(own)}
    for k in early:
        blocks[k, 0, FIRST] = shift_ring(first_half[0], k)
    total = None
    for n, group in enumerate(groups):
        if n > 0:
            for name in group:
                (blocks[name],) = gate([token], [blocks[name]])
        if n == 1:
            for k in early:
                blocks[k, 0, SECOND] = swap_occ(blocks[k, 0, FIRST], 2)
                blocks[k, 1, FIRST] = swap_pair(blocks[k, 0, FIRST])
            for k in late:
                near, step = (k - reach, reach) if k - reach in early else (k + reach, -reach)
                blocks[k, 0, FIRST] = shift_ring(blocks[near, 0, FIRST], step)
        if n == 2:
            for k in odd:
                (blocks[k, 1, FIRST],) = gate([token], [blocks[k, 1, FIRST]])
            for k in late:
                blocks[k, 0, SECOND] = swap_occ(blocks[k, 0, FIRST], 2)
                blocks[k, 1, FIRST] = swap_pair(blocks[k, 0, FIRST])
            for k in even:
                blocks[k, 1, SECOND] = swap_pair(blocks[k, 0, SECOND])
            for k in odd:
                blocks[k, 1, SECOND] = swap_occ(blocks[k, 1, FIRST], 2)
        if n == 3:
            for k in late:
                blocks[k, 1, SECOND] = swap_pair(blocks[k, 0, SECOND])
        pairs = [block for name in group for block in (blocks[name], swap_occ(blocks[name], 1))]
        total, token = contract(rows, row_energy, energies[n], pairs, total, n == len(groups) - 1)
    return total.reshape(integrals.shape)


def solution(mesh):
    in_specs = (P("occ", "virt", None), P(), P(), P())
    out_specs = P("occ", "virt", None)

    def run(integrals, occ_energy, virt_energy, partners):
        return per_device(
            mesh.shape["occ"], mesh.shape["virt"], integrals, occ_energy, virt_energy, partners
        )

    return jax.shard_map(run, mesh=mesh, in_specs=in_specs, out_specs=out_specs, check_vma=False)
```

```python
import jax
import jax.numpy as jnp
from jax import lax
from jax.experimental import pallas as pl
from jax.experimental.pallas import tpu as pltpu
from jax.sharding import PartitionSpec as P

FIRST, SECOND = range(2)

VMEM = pl.BlockSpec(memory_space=pltpu.VMEM)
SMEM = pl.BlockSpec(memory_space=pltpu.SMEM)
ANY = pl.BlockSpec(memory_space=pl.ANY)
TOKEN = jax.ShapeDtypeStruct((8, 128), jnp.float32)


def call(kernel, operands, in_specs, outs, scratch=(), aliases=None, vmem=2):
    return pl.pallas_call(
        kernel,
        in_specs=in_specs,
        out_specs=[spec for spec, _ in outs],
        out_shape=[shape for _, shape in outs],
        scratch_shapes=list(scratch),
        input_output_aliases=aliases or {},
        compiler_params=pltpu.CompilerParams(vmem_limit_bytes=vmem << 20),
        cost_estimate=pl.CostEstimate(flops=0, bytes_accessed=0, transcendentals=0),
    )(*operands)


def extract(bits, partners, integrals):
    occ_dev = integrals.shape[0]
    shape = pltpu.VMEM(integrals.shape[1:], integrals.dtype)

    def kernel(partners_ref, integrals_ref, own_ref, sent_ref, held_ref, sems):
        occ_index = lax.axis_index("occ")
        core = lax.rem(occ_index, 2)
        copies = []
        for k, (out_ref, step) in enumerate(((sent_ref, 1 - core), (own_ref, core))):
            row = lax.rem(partners_ref[step], occ_dev)
            copies.append(pltpu.make_async_copy(integrals_ref.at[row], out_ref, sems.at[k]))
        for copy in copies:
            copy.start()
        owner = lax.div(partners_ref[core], occ_dev)
        for k, bit in enumerate(bits):
            held = jnp.where(lax.div(owner, bit) == lax.div(occ_index, bit), 1, 0)
            held_ref[pl.ds(8 * k, 8), :] = jnp.full((8, 128), held, jnp.int32)
        for copy in copies:
            copy.wait()

    flags = pltpu.VMEM((8 * len(bits), 128), jnp.int32)
    return call(
        kernel,
        [partners, integrals],
        [SMEM, ANY],
        [(VMEM, shape), (VMEM, shape), (VMEM, flags)],
        [pltpu.SemaphoreType.DMA((2,))],
        vmem=56,
    )


def choose(held, n, own, got, token=None):
    halves = 2 if n == 0 else 1
    depth, width = own.shape[0] // halves, own.shape[1]

    def kernel(held_ref, own_ref, got_ref, *rest):
        out_refs = rest[-halves:]
        plane = lax.rem(lax.div(lax.axis_index("occ"), 2), 2)
        flag = held_ref[8 * n : 8 * n + 1, 0:1] == 1
        for k in range(halves):
            at = pl.multiple_of(lax.rem(plane + k, 2) * depth, depth) if halves == 2 else 0
            rows = pl.ds(at, depth)
            out_refs[k][...] = jnp.where(flag, own_ref[rows, :], got_ref[rows, :])

    operands, specs = [held, own, got], [VMEM] * 3
    if token is not None:
        operands.append(token)
        specs.append(ANY)
    return call(kernel, operands, specs, [(VMEM, pltpu.VMEM((depth, width), own.dtype))] * halves)


def prepare(where, partners, occ_energy, column, virt_halves, rows, groups, ready):
    height = rows.shape[0]
    local_virt, half = column.shape[0], virt_halves.shape[1]
    occ_dev, virt_size = height // local_virt, virt_halves.shape[0] // 2
    widths = [half * len(places) for places in groups]

    def kernel(where_ref, partners_ref, occ_energy_ref, column_ref, virt_ref, rows_ref, *rest):
        rest = rest[1:]
        out_ref, row_energy_ref, token_ref = rest[:3]
        energy_refs, sem = rest[3:-1], rest[-1]
        load = pltpu.make_async_copy(rows_ref, out_ref, sem)
        load.start()
        virt_index, occ_index = where_ref[0], where_ref[1]
        plane = lax.rem(lax.div(occ_index, 2), 2)
        token_ref[...] = jnp.zeros_like(token_ref)
        for i in range(occ_dev):
            own = occ_energy_ref[occ_index * occ_dev + i]
            row_energy_ref[pl.ds(i * local_virt, local_virt), :] = column_ref[...] - own
        for places, energy_ref in zip(groups, energy_refs):
            for k, (ring_step, side, which, step) in enumerate(places):
                position = lax.rem(virt_index + 2 * ring_step, virt_size)
                position = position + side * (1 - 2 * lax.rem(position, 2))
                pair = occ_energy_ref[partners_ref[lax.rem(occ_index + step, 2)]]
                part = lax.rem(plane + which, 2)
                energy_ref[:, k * half : (k + 1) * half] = virt_ref[pl.ds(2 * position + part, 1), :] - pair
        load.wait()

    outs = [(VMEM, pltpu.VMEM(rows.shape, rows.dtype)), (VMEM, pltpu.VMEM((height, 1), jnp.float32)), (VMEM, TOKEN)]
    outs += [(VMEM, pltpu.VMEM((1, width), jnp.float32)) for width in widths]
    rows, row_energy, token, *energies = call(
        kernel,
        [where, partners, occ_energy, column, virt_halves, rows, ready],
        [SMEM] * 3 + [VMEM] * 2 + [ANY] * 2,
        outs,
        [pltpu.SemaphoreType.DMA],
        vmem=16,
    )
    return rows, row_energy, token, energies


def contract(rows, row_energy, block_energy, blocks, waits, total, last):
    height, width = rows.shape
    count, depths = len(blocks), [block.shape[0] for block in blocks]
    starts, depth = [sum(depths[:k]) for k in range(count)], sum(depths)
    tile = max(t for t in range(16, 513, 16) if height % t == 0)
    tiles = height // tile

    def kernel(rows_ref, row_energy_ref, block_energy_ref, *rest):
        block_refs, rest = rest[:count], rest[count + len(waits) :]
        total_ref, rest = (rest[0], rest[1:]) if total is not None else (None, rest)
        out_ref, token_ref, held, sems = rest[:4]
        copies = [
            pltpu.make_async_copy(block_refs[k], held.at[pl.ds(starts[k], depths[k])], sems.at[k])
            for k in range(count)
        ]
        for copy in copies:
            copy.start()
        token_ref[...] = jnp.zeros_like(token_ref)
        for copy in copies:
            copy.wait()
        writes = []
        for i in range(tiles):
            at = pl.ds(i * tile, tile)
            scores = lax.dot_general(
                rows_ref[at, :], held[...], (((1,), (1,)), ((), ())), preferred_element_type=jnp.float32
            )
            amplitudes = (scores / (row_energy_ref[at, :] + block_energy_ref[...])).astype(jnp.bfloat16)
            result = jnp.dot(amplitudes, held[...], preferred_element_type=jnp.float32)
            if total_ref is not None:
                result = result + total_ref[at, :]
            if last:
                staged, write_sems = rest[4:]
                if i >= 2:
                    writes[i - 2].wait()
                staged[i % 2] = result.astype(jnp.bfloat16)
                write = pltpu.make_async_copy(staged.at[i % 2], out_ref.at[at, :], write_sems.at[i])
                write.start()
                writes.append(write)
            else:
                out_ref[at, :] = result
        for write in writes[-2:]:
            write.wait()

    operands = [rows, row_energy, block_energy, *blocks, *waits]
    specs = [VMEM] * 3 + [ANY] * (count + len(waits))
    if total is not None:
        operands.append(total)
        specs.append(VMEM)
    scratch = [pltpu.VMEM((depth, width), jnp.bfloat16), pltpu.SemaphoreType.DMA((count,))]
    if last:
        scratch += [pltpu.VMEM((2, tile, width), jnp.bfloat16), pltpu.SemaphoreType.DMA((tiles,))]
        out = (ANY, jax.ShapeDtypeStruct((height, width), jnp.bfloat16))
    else:
        out = (VMEM, pltpu.VMEM((height, width), jnp.float32))
    aliases = {len(operands) - 1: 0} if total is not None and not last else {}
    return call(kernel, operands, specs, [out, (VMEM, TOKEN)], scratch, aliases, vmem=16)


def gate(tokens, values):
    skip = len(tokens)

    def kernel(*refs):
        del refs

    outs = [(ANY, jax.ShapeDtypeStruct(value.shape, value.dtype)) for value in values]
    aliases = {skip + k: k for k in range(len(values))}
    return call(kernel, [*tokens, *values], [ANY] * (skip + len(values)), outs, aliases=aliases, vmem=1)


def per_device(occ_size, virt_size, integrals, occ_energy, virt_energy, partners):
    occ_dev, local_virt, aux_width = integrals.shape
    occ_index, virt_index = lax.axis_index("occ"), lax.axis_index("virt")
    ring, half = virt_size // 2, local_virt // 2

    def swap_occ(value, bit):
        return lax.ppermute(value, "occ", [(o, o ^ bit) for o in range(occ_size)])

    def swap_pair(value):
        return lax.ppermute(value, "virt", [(v, v ^ 1) for v in range(virt_size)])

    def shift_ring(value, k):
        return lax.ppermute(value, "virt", [(v, (v - 2 * k) % virt_size) for v in range(virt_size)])

    shifts = sorted(range(1, ring), key=lambda k: min(k, ring - k))
    early, late = shifts[: ring // 2], shifts[ring // 2 :]
    even, odd, reach = early[0::2], early[1::2], (len(early) + 1) // 2
    groups = [
        [(0, 0, FIRST)],
        [(0, 0, SECOND), (0, 1, FIRST)] + [(k, 0, FIRST) for k in early],
        [(k, 0, FIRST) for k in late] + [(k, 0, SECOND) for k in early] + [(k, 1, FIRST) for k in odd],
        [(k, 0, SECOND) for k in late] + [(k, 1, FIRST) for k in late + even] + [(0, 1, SECOND)],
        [(k, 1, SECOND) for k in early + late],
    ]
    awaited = [[(0, 0, SECOND)], [], [(0, 1, SECOND)], [(k, 1, SECOND) for k in early], []]
    places = [[(*place, step) for place in group for step in range(2)] for group in groups]

    where = jnp.stack([virt_index, occ_index]).astype(jnp.int32)
    column = lax.dynamic_slice_in_dim(virt_energy, virt_index * local_virt, local_virt)[:, None]
    virt_halves = virt_energy.reshape(2 * virt_size, half)
    bits = [1 << n for n in range(occ_size.bit_length() - 1)]
    own, sent, held = extract(bits, partners, integrals)
    first, second = choose(held, 0, own, swap_occ(sent, 1))
    rows, row_energy, token, energies = prepare(
        where, partners, occ_energy, column, virt_halves, integrals.reshape(-1, aux_width), places, first
    )
    sent = [second, first]
    for n, bit in list(enumerate(bits))[1:]:
        (first,) = choose(held, n, first, swap_occ(sent[0] if bit == 2 else first, bit), token)
    blocks = {(0, 0, FIRST): first, (0, 1, FIRST): swap_pair(first)}
    for k in early:
        blocks[k, 0, FIRST] = shift_ring(first, k)
    for n, bit in list(enumerate(bits))[1:]:
        got = swap_occ(sent[1] if bit == 2 else second, bit)
        (second,) = choose(held, n, second, got, token)
    blocks[0, 0, SECOND] = second
    total = None
    for n, group in enumerate(groups):
        if n > 0:
            for name in [*group, *awaited[n]]:
                if n == 1 or name not in awaited[n - 1]:
                    (blocks[name],) = gate([token], [blocks[name]])
        if n == 1:
            for k in late:
                near, step = (k - reach, reach) if k - reach in early else (k + reach, -reach)
                blocks[k, 0, FIRST] = shift_ring(blocks[near, 0, FIRST], step)
            for k in early:
                blocks[k, 0, SECOND] = swap_occ(blocks[k, 0, FIRST], 2)
            for k in odd:
                blocks[k, 1, FIRST] = swap_pair(blocks[k, 0, FIRST])
            for k in even:
                blocks[k, 1, FIRST] = shift_ring(blocks[0, 1, FIRST], k)
            blocks[0, 1, SECOND] = swap_pair(blocks[0, 0, SECOND])
        if n == 2:
            for k in late:
                blocks[k, 0, SECOND] = swap_occ(blocks[k, 0, FIRST], 2)
                blocks[k, 1, FIRST] = swap_pair(blocks[k, 0, FIRST])
            for k in even:
                blocks[k, 1, SECOND] = swap_pair(blocks[k, 0, SECOND])
            for k in odd:
                blocks[k, 1, SECOND] = swap_occ(blocks[k, 1, FIRST], 2)
        if n == 3:
            for k in late:
                blocks[k, 1, SECOND] = swap_pair(blocks[k, 0, SECOND])
        pairs = [block for name in group for block in (blocks[name], swap_occ(blocks[name], 1))]
        waits = [blocks[name] for name in awaited[n]]
        total, token = contract(rows, row_energy, energies[n], pairs, waits, total, n == len(groups) - 1)
    return total.reshape(integrals.shape)


def solution(mesh):
    in_specs = (P("occ", "virt", None), P(), P(), P())
    out_specs = P("occ", "virt", None)

    def run(integrals, occ_energy, virt_energy, partners):
        return per_device(
            mesh.shape["occ"], mesh.shape["virt"], integrals, occ_energy, virt_energy, partners
        )

    return jax.shard_map(run, mesh=mesh, in_specs=in_specs, out_specs=out_specs, check_vma=False)
```

```python
import jax
import jax.numpy as jnp
from jax import lax
from jax.experimental import pallas as pl
from jax.experimental.pallas import tpu as pltpu
from jax.sharding import PartitionSpec as P

FIRST, SECOND = range(2)

VMEM = pl.BlockSpec(memory_space=pltpu.VMEM)
SMEM = pl.BlockSpec(memory_space=pltpu.SMEM)
ANY = pl.BlockSpec(memory_space=pl.ANY)
TOKEN = jax.ShapeDtypeStruct((8, 128), jnp.float32)


def call(kernel, operands, in_specs, outs, scratch=(), aliases=None, vmem=2):
    return pl.pallas_call(
        kernel,
        in_specs=in_specs,
        out_specs=[spec for spec, _ in outs],
        out_shape=[shape for _, shape in outs],
        scratch_shapes=list(scratch),
        input_output_aliases=aliases or {},
        compiler_params=pltpu.CompilerParams(vmem_limit_bytes=vmem << 20),
        cost_estimate=pl.CostEstimate(flops=0, bytes_accessed=0, transcendentals=0),
    )(*operands)


def padded(depth):
    return depth if depth <= 256 else -(-depth // 256) * 256


def extract(bits, partners, integrals):
    occ_dev = integrals.shape[0]
    shape = pltpu.VMEM(integrals.shape[1:], integrals.dtype)

    def kernel(partners_ref, integrals_ref, own_ref, sent_ref, held_ref, sems):
        occ_index = lax.axis_index("occ")
        core = lax.rem(occ_index, 2)
        copies = []
        for k, (out_ref, step) in enumerate(((sent_ref, 1 - core), (own_ref, core))):
            row = lax.rem(partners_ref[step], occ_dev)
            copies.append(pltpu.make_async_copy(integrals_ref.at[row], out_ref, sems.at[k]))
        for copy in copies:
            copy.start()
        owner = lax.div(partners_ref[core], occ_dev)
        for k, bit in enumerate(bits):
            held = jnp.where(lax.div(owner, bit) == lax.div(occ_index, bit), 1, 0)
            held_ref[pl.ds(8 * k, 8), :] = jnp.full((8, 128), held, jnp.int32)
        for copy in copies:
            copy.wait()

    flags = pltpu.VMEM((8 * len(bits), 128), jnp.int32)
    return call(
        kernel,
        [partners, integrals],
        [SMEM, ANY],
        [(VMEM, shape), (VMEM, shape), (VMEM, flags)],
        [pltpu.SemaphoreType.DMA((2,))],
        vmem=56,
    )


def choose(held, n, own, got, token=None):
    halves = 2 if n == 0 else 1
    depth, width = own.shape[0] // halves, own.shape[1]

    def kernel(held_ref, own_ref, got_ref, *rest):
        out_refs = rest[-halves:]
        plane = lax.rem(lax.div(lax.axis_index("occ"), 2), 2)
        flag = held_ref[8 * n : 8 * n + 1, 0:1] == 1
        for k in range(halves):
            at = pl.multiple_of(lax.rem(plane + k, 2) * depth, depth) if halves == 2 else 0
            rows = pl.ds(at, depth)
            out_refs[k][...] = jnp.where(flag, own_ref[rows, :], got_ref[rows, :])

    operands, specs = [held, own, got], [VMEM] * 3
    if token is not None:
        operands.append(token)
        specs.append(ANY)
    return call(kernel, operands, specs, [(VMEM, pltpu.VMEM((depth, width), own.dtype))] * halves)


def pick(first, second):
    def kernel(first_ref, second_ref, out_ref):
        core = lax.rem(lax.axis_index("occ"), 2)
        flag = jnp.full((1, 1), core, jnp.int32) == 0
        out_ref[...] = jnp.where(flag, first_ref[...], second_ref[...])

    outs = [(VMEM, pltpu.VMEM(first.shape, first.dtype))]
    return call(kernel, [first, second], [VMEM, VMEM], outs)[0]


def prepare(where, partners, occ_energy, column, virt_halves, rows, groups, ready):
    height = rows.shape[0]
    local_virt, half = column.shape[0], virt_halves.shape[1]
    occ_dev, virt_size = height // local_virt, virt_halves.shape[0] // 2
    widths = [padded(half * len(places)) for places in groups]

    def kernel(where_ref, partners_ref, occ_energy_ref, column_ref, virt_ref, rows_ref, *rest):
        rest = rest[1:]
        out_ref, row_energy_ref, token_ref = rest[:3]
        energy_refs, sem = rest[3:-1], rest[-1]
        load = pltpu.make_async_copy(rows_ref, out_ref, sem)
        load.start()
        virt_index, occ_index = where_ref[0], where_ref[1]
        plane = lax.rem(lax.div(occ_index, 2), 2)
        token_ref[...] = jnp.zeros_like(token_ref)
        for i in range(occ_dev):
            own = occ_energy_ref[occ_index * occ_dev + i]
            row_energy_ref[pl.ds(i * local_virt, local_virt), :] = column_ref[...] - own
        for places, energy_ref in zip(groups, energy_refs):
            energy_ref[...] = jnp.ones_like(energy_ref)
            for k, (ring_step, side, which, step) in enumerate(places):
                position = lax.rem(virt_index + 2 * ring_step, virt_size)
                position = position + side * (1 - 2 * lax.rem(position, 2))
                pair = occ_energy_ref[partners_ref[lax.rem(occ_index + step, 2)]]
                part = lax.rem(plane + which, 2)
                energy_ref[:, k * half : (k + 1) * half] = virt_ref[pl.ds(2 * position + part, 1), :] - pair
        load.wait()

    outs = [(VMEM, pltpu.VMEM(rows.shape, rows.dtype)), (VMEM, pltpu.VMEM((height, 1), jnp.float32)), (VMEM, TOKEN)]
    outs += [(VMEM, pltpu.VMEM((1, width), jnp.float32)) for width in widths]
    rows, row_energy, token, *energies = call(
        kernel,
        [where, partners, occ_energy, column, virt_halves, rows, ready],
        [SMEM] * 3 + [VMEM] * 2 + [ANY] * 2,
        outs,
        [pltpu.SemaphoreType.DMA],
        vmem=16,
    )
    return rows, row_energy, token, energies


def contract(rows, row_energy, block_energy, blocks, waits, total, last):
    height, width = rows.shape
    count, depths = len(blocks), [block.shape[0] for block in blocks]
    starts, depth = [sum(depths[:k]) for k in range(count)], padded(sum(depths))
    tile = max(t for t in range(16, 513, 16) if height % t == 0)
    tiles = height // tile

    def kernel(rows_ref, row_energy_ref, block_energy_ref, *rest):
        block_refs, rest = rest[:count], rest[count + len(waits) :]
        total_ref, rest = (rest[0], rest[1:]) if total is not None else (None, rest)
        out_ref, token_ref, held, sems = rest[:4]
        copies = [
            pltpu.make_async_copy(block_refs[k], held.at[pl.ds(starts[k], depths[k])], sems.at[k])
            for k in range(count)
        ]
        for copy in copies:
            copy.start()
        token_ref[...] = jnp.zeros_like(token_ref)
        if sum(depths) < depth:
            held[sum(depths) :, :] = jnp.zeros((depth - sum(depths), width), held.dtype)
        for copy in copies:
            copy.wait()
        writes = []
        for i in range(tiles):
            at = pl.ds(i * tile, tile)
            scores = lax.dot_general(
                rows_ref[at, :], held[...], (((1,), (1,)), ((), ())), preferred_element_type=jnp.float32
            )
            amplitudes = (scores / (row_energy_ref[at, :] + block_energy_ref[...])).astype(jnp.bfloat16)
            result = jnp.dot(amplitudes, held[...], preferred_element_type=jnp.float32)
            if total_ref is not None:
                result = result + total_ref[at, :]
            if last:
                staged, write_sems = rest[4:]
                if i >= 2:
                    writes[i - 2].wait()
                staged[i % 2] = result.astype(jnp.bfloat16)
                write = pltpu.make_async_copy(staged.at[i % 2], out_ref.at[at, :], write_sems.at[i])
                write.start()
                writes.append(write)
            else:
                out_ref[at, :] = result
        for write in writes[-2:]:
            write.wait()

    operands = [rows, row_energy, block_energy, *blocks, *waits]
    specs = [VMEM] * 3 + [ANY] * (count + len(waits))
    if total is not None:
        operands.append(total)
        specs.append(VMEM)
    scratch = [pltpu.VMEM((depth, width), jnp.bfloat16), pltpu.SemaphoreType.DMA((count,))]
    if last:
        scratch += [pltpu.VMEM((2, tile, width), jnp.bfloat16), pltpu.SemaphoreType.DMA((tiles,))]
        out = (ANY, jax.ShapeDtypeStruct((height, width), jnp.bfloat16))
    else:
        out = (VMEM, pltpu.VMEM((height, width), jnp.float32))
    aliases = {len(operands) - 1: 0} if total is not None and not last else {}
    return call(kernel, operands, specs, [out, (VMEM, TOKEN)], scratch, aliases, vmem=16)


def gate(tokens, values):
    skip = len(tokens)

    def kernel(*refs):
        del refs

    outs = [(ANY, jax.ShapeDtypeStruct(value.shape, value.dtype)) for value in values]
    aliases = {skip + k: k for k in range(len(values))}
    return call(kernel, [*tokens, *values], [ANY] * (skip + len(values)), outs, aliases=aliases, vmem=1)


def per_device(occ_size, virt_size, integrals, occ_energy, virt_energy, partners):
    occ_dev, local_virt, aux_width = integrals.shape
    occ_index, virt_index = lax.axis_index("occ"), lax.axis_index("virt")
    ring, half = virt_size // 2, local_virt // 2

    def swap_occ(value, bit):
        return lax.ppermute(value, "occ", [(o, o ^ bit) for o in range(occ_size)])

    def swap_pair(value):
        return lax.ppermute(value, "virt", [(v, v ^ 1) for v in range(virt_size)])

    def shift_ring(value, k):
        return lax.ppermute(value, "virt", [(v, (v - 2 * k) % virt_size) for v in range(virt_size)])

    def mix(value):
        to = [(o ^ 2, v) if o % 2 == 0 else (o, v ^ 1) for o in range(occ_size) for v in range(virt_size)]
        moves = [(n, o * virt_size + v) for n, (o, v) in enumerate(to)]
        return lax.ppermute(value, ("occ", "virt"), moves)

    shifts = sorted(range(1, ring), key=lambda k: min(k, ring - k))
    early, late = shifts[: ring // 2], shifts[ring // 2 :]
    kinds = {"O": [0], "A": early[0::2], "B": early[1::2], "C": late}
    reach = (len(early) + 1) // 2
    plan = {
        ("C", 0, SECOND): ("plane", 3, 3),
        ("A", 1, SECOND): ("both", 4, 4),
        ("A", 0, FIRST): ("ring", 1, 1),
        ("O", 0, FIRST): ("own", 0, 1),
        ("O", 1, SECOND): ("both", 2, 3),
        ("B", 1, FIRST): ("shift", 3, 3),
        ("B", 1, SECOND): ("both", 4, 4),
        ("B", 0, SECOND): ("plane", 3, 4),
        ("C", 0, FIRST): ("ring", 2, 2),
        ("C", 1, FIRST): ("pair", 3, 3),
        ("A", 0, SECOND): ("plane", 2, 2),
        ("A", 1, FIRST): ("pair", 2, 2),
        ("B", 0, FIRST): ("ring", 2, 2),
        ("O", 0, SECOND): ("own", 1, 1),
        ("O", 1, FIRST): ("pair", 1, 1),
        ("C", 1, SECOND): ("both", 4, 4),
    }
    listed = [((k, side, half), *plan[kind, side, half]) for kind, side, half in plan for k in kinds[kind]]
    stages = 1 + max(group for *_, group in listed)
    groups = [[name for name, _, _, group in listed if group == n] for n in range(stages)]
    places = [[(*name, step) for name in group for step in range(2)] for group in groups]

    where = jnp.stack([virt_index, occ_index]).astype(jnp.int32)
    column = lax.dynamic_slice_in_dim(virt_energy, virt_index * local_virt, local_virt)[:, None]
    virt_halves = virt_energy.reshape(2 * virt_size, half)
    bits = [1 << n for n in range(occ_size.bit_length() - 1)]
    own, sent, held = extract(bits, partners, integrals)
    first, second = choose(held, 0, own, swap_occ(sent, 1))
    rows, row_energy, token, energies = prepare(
        where, partners, occ_energy, column, virt_halves, integrals.reshape(-1, aux_width), [group for group in places if group], first
    )
    sent = [second, first]
    for n, bit in list(enumerate(bits))[1:]:
        (first,) = choose(held, n, first, swap_occ(sent[0] if bit == 2 else first, bit), token)
    for n, bit in list(enumerate(bits))[1:]:
        got = swap_occ(sent[1] if bit == 2 else second, bit)
        (second,) = choose(held, n, second, got, token)

    blocks = {(0, 0, FIRST): first}

    def fetch(name, move):
        k, side, half = name
        if move == "own":
            return second
        if move == "ring":
            near = k - reach if (k - reach, 0, FIRST) in blocks else 0
            return shift_ring(blocks[near, 0, FIRST], k - near)
        if move == "plane":
            return swap_occ(blocks[k, side, FIRST], 2)
        if move == "pair":
            return swap_pair(blocks[k, 0, half])
        if move == "both":
            return mix(pick(blocks[k, 1, FIRST], blocks[k, 0, SECOND]))
        return shift_ring(blocks[0, side, half], k)

    fetched, total = {}, None
    for n in range(stages):
        for name, move, stage, _ in listed:
            if stage == n == 0 and name != (0, 0, FIRST):
                blocks[name] = fetch(name, move)
            if stage == n > 0:
                (blocks[name],) = gate([token], [fetched[name]])
        for name, move, stage, _ in listed:
            if stage == n + 1:
                fetched[name] = fetch(name, move)
        if not groups[n]:
            continue
        pairs = [block for name in groups[n] for block in (blocks[name], swap_occ(blocks[name], 1))]
        waits = [second] if n == 0 else [blocks[name] for name, _, stage, _ in listed if stage == n and name not in groups[n]]
        total, token = contract(rows, row_energy, energies.pop(0), pairs, waits, total, n == stages - 1)
    return total.reshape(integrals.shape)


def solution(mesh):
    in_specs = (P("occ", "virt", None), P(), P(), P())
    out_specs = P("occ", "virt", None)

    def run(integrals, occ_energy, virt_energy, partners):
        return per_device(
            mesh.shape["occ"], mesh.shape["virt"], integrals, occ_energy, virt_energy, partners
        )

    return jax.shard_map(run, mesh=mesh, in_specs=in_specs, out_specs=out_specs, check_vma=False)
```

```python
import jax
import jax.numpy as jnp
from jax import lax
from jax.experimental import pallas as pl
from jax.experimental.pallas import tpu as pltpu
from jax.sharding import PartitionSpec as P

FIRST, SECOND = range(2)

VMEM = pl.BlockSpec(memory_space=pltpu.VMEM)
SMEM = pl.BlockSpec(memory_space=pltpu.SMEM)
ANY = pl.BlockSpec(memory_space=pl.ANY)
TOKEN = jax.ShapeDtypeStruct((8, 128), jnp.float32)


def call(kernel, operands, in_specs, outs, scratch=(), aliases=None, vmem=2):
    return pl.pallas_call(
        kernel,
        in_specs=in_specs,
        out_specs=[spec for spec, _ in outs],
        out_shape=[shape for _, shape in outs],
        scratch_shapes=list(scratch),
        input_output_aliases=aliases or {},
        compiler_params=pltpu.CompilerParams(vmem_limit_bytes=vmem << 20),
        cost_estimate=pl.CostEstimate(flops=0, bytes_accessed=0, transcendentals=0),
    )(*operands)


def padded(depth):
    return depth if depth <= 256 else -(-depth // 256) * 256


def extract(bits, partners, integrals):
    occ_dev = integrals.shape[0]
    shape = pltpu.VMEM(integrals.shape[1:], integrals.dtype)

    def kernel(partners_ref, integrals_ref, own_ref, sent_ref, held_ref, sems):
        occ_index = lax.axis_index("occ")
        core = lax.rem(occ_index, 2)
        copies = []
        for k, (out_ref, step) in enumerate(((sent_ref, 1 - core), (own_ref, core))):
            row = lax.rem(partners_ref[step], occ_dev)
            copies.append(pltpu.make_async_copy(integrals_ref.at[row], out_ref, sems.at[k]))
        for copy in copies:
            copy.start()
        owner = lax.div(partners_ref[core], occ_dev)
        for k, bit in enumerate(bits):
            held = jnp.where(lax.div(owner, bit) == lax.div(occ_index, bit), 1, 0)
            held_ref[pl.ds(8 * k, 8), :] = jnp.full((8, 128), held, jnp.int32)
        for copy in copies:
            copy.wait()

    flags = pltpu.VMEM((8 * len(bits), 128), jnp.int32)
    return call(
        kernel,
        [partners, integrals],
        [SMEM, ANY],
        [(VMEM, shape), (VMEM, shape), (VMEM, flags)],
        [pltpu.SemaphoreType.DMA((2,))],
        vmem=56,
    )


def choose(held, n, own, got, token=None):
    halves = 2 if n == 0 else 1
    depth, width = own.shape[0] // halves, own.shape[1]

    def kernel(held_ref, own_ref, got_ref, *rest):
        out_refs = rest[-halves:]
        plane = lax.rem(lax.div(lax.axis_index("occ"), 2), 2)
        flag = held_ref[8 * n : 8 * n + 1, 0:1] == 1
        for k in range(halves):
            at = pl.multiple_of(lax.rem(plane + k, 2) * depth, depth) if halves == 2 else 0
            rows = pl.ds(at, depth)
            out_refs[k][...] = jnp.where(flag, own_ref[rows, :], got_ref[rows, :])

    operands, specs = [held, own, got], [VMEM] * 3
    if token is not None:
        operands.append(token)
        specs.append(ANY)
    return call(kernel, operands, specs, [(VMEM, pltpu.VMEM((depth, width), own.dtype))] * halves)


def pick(first, second):
    def kernel(first_ref, second_ref, out_ref):
        core = lax.rem(lax.axis_index("occ"), 2)
        flag = jnp.full((1, 1), core, jnp.int32) == 0
        out_ref[...] = jnp.where(flag, first_ref[...], second_ref[...])

    outs = [(VMEM, pltpu.VMEM(first.shape, first.dtype))]
    return call(kernel, [first, second], [VMEM, VMEM], outs)[0]


def prepare(where, partners, occ_energy, column, virt_halves, rows, groups, ready):
    height = rows.shape[0]
    local_virt, half = column.shape[0], virt_halves.shape[1]
    occ_dev, virt_size = height // local_virt, virt_halves.shape[0] // 2
    widths = [padded(half * len(places)) for places in groups]

    def kernel(where_ref, partners_ref, occ_energy_ref, column_ref, virt_ref, rows_ref, *rest):
        rest = rest[1:]
        out_ref, row_energy_ref, token_ref = rest[:3]
        energy_refs, sem = rest[3:-1], rest[-1]
        load = pltpu.make_async_copy(rows_ref, out_ref, sem)
        load.start()
        virt_index, occ_index = where_ref[0], where_ref[1]
        plane = lax.rem(lax.div(occ_index, 2), 2)
        token_ref[...] = jnp.zeros_like(token_ref)
        for i in range(occ_dev):
            own = occ_energy_ref[occ_index * occ_dev + i]
            row_energy_ref[pl.ds(i * local_virt, local_virt), :] = column_ref[...] - own
        for places, energy_ref in zip(groups, energy_refs):
            energy_ref[...] = jnp.ones_like(energy_ref)
            for k, (ring_step, side, which, step) in enumerate(places):
                position = lax.rem(virt_index + 2 * ring_step, virt_size)
                position = position + side * (1 - 2 * lax.rem(position, 2))
                pair = occ_energy_ref[partners_ref[lax.rem(occ_index + step, 2)]]
                part = lax.rem(plane + which, 2)
                energy_ref[:, k * half : (k + 1) * half] = virt_ref[pl.ds(2 * position + part, 1), :] - pair
        load.wait()

    outs = [(VMEM, pltpu.VMEM(rows.shape, rows.dtype)), (VMEM, pltpu.VMEM((height, 1), jnp.float32)), (VMEM, TOKEN)]
    outs += [(VMEM, pltpu.VMEM((1, width), jnp.float32)) for width in widths]
    rows, row_energy, token, *energies = call(
        kernel,
        [where, partners, occ_energy, column, virt_halves, rows, ready],
        [SMEM] * 3 + [VMEM] * 2 + [ANY] * 2,
        outs,
        [pltpu.SemaphoreType.DMA],
        vmem=16,
    )
    return rows, row_energy, token, energies


def contract(rows, row_energy, block_energy, blocks, waits, total, last):
    height, width = rows.shape
    count, depths = len(blocks), [block.shape[0] for block in blocks]
    starts, depth = [sum(depths[:k]) for k in range(count)], padded(sum(depths))
    tile = max(t for t in range(16, 513, 16) if height % t == 0)
    tiles = height // tile

    def kernel(rows_ref, row_energy_ref, block_energy_ref, *rest):
        block_refs, rest = rest[:count], rest[count + len(waits) :]
        total_ref, rest = (rest[0], rest[1:]) if total is not None else (None, rest)
        out_ref, token_ref, held, sems = rest[:4]
        copies = [
            pltpu.make_async_copy(block_refs[k], held.at[pl.ds(starts[k], depths[k])], sems.at[k])
            for k in range(count)
        ]
        for copy in copies:
            copy.start()
        token_ref[...] = jnp.zeros_like(token_ref)
        if sum(depths) < depth:
            held[sum(depths) :, :] = jnp.zeros((depth - sum(depths), width), held.dtype)
        for copy in copies:
            copy.wait()
        writes = []
        for i in range(tiles):
            at = pl.ds(i * tile, tile)
            scores = lax.dot_general(
                rows_ref[at, :], held[...], (((1,), (1,)), ((), ())), preferred_element_type=jnp.float32
            )
            amplitudes = (scores / (row_energy_ref[at, :] + block_energy_ref[...])).astype(jnp.bfloat16)
            result = jnp.dot(amplitudes, held[...], preferred_element_type=jnp.float32)
            if total_ref is not None:
                result = result + total_ref[at, :]
            if last:
                staged, write_sems = rest[4:]
                if i >= 2:
                    writes[i - 2].wait()
                staged[i % 2] = result.astype(jnp.bfloat16)
                write = pltpu.make_async_copy(staged.at[i % 2], out_ref.at[at, :], write_sems.at[i])
                write.start()
                writes.append(write)
            else:
                out_ref[at, :] = result
        for write in writes[-2:]:
            write.wait()

    operands = [rows, row_energy, block_energy, *blocks, *waits]
    specs = [VMEM] * 3 + [ANY] * (count + len(waits))
    if total is not None:
        operands.append(total)
        specs.append(VMEM)
    scratch = [pltpu.VMEM((depth, width), jnp.bfloat16), pltpu.SemaphoreType.DMA((count,))]
    if last:
        scratch += [pltpu.VMEM((2, tile, width), jnp.bfloat16), pltpu.SemaphoreType.DMA((tiles,))]
        out = (ANY, jax.ShapeDtypeStruct((height, width), jnp.bfloat16))
    else:
        out = (VMEM, pltpu.VMEM((height, width), jnp.float32))
    aliases = {len(operands) - 1: 0} if total is not None and not last else {}
    return call(kernel, operands, specs, [out, (VMEM, TOKEN)], scratch, aliases, vmem=16)


def gate(tokens, values):
    skip = len(tokens)

    def kernel(*refs):
        del refs

    outs = [(ANY, jax.ShapeDtypeStruct(value.shape, value.dtype)) for value in values]
    aliases = {skip + k: k for k in range(len(values))}
    return call(kernel, [*tokens, *values], [ANY] * (skip + len(values)), outs, aliases=aliases, vmem=1)


def per_device(occ_size, virt_size, integrals, occ_energy, virt_energy, partners):
    occ_dev, local_virt, aux_width = integrals.shape
    occ_index, virt_index = lax.axis_index("occ"), lax.axis_index("virt")
    ring, half = virt_size // 2, local_virt // 2

    def swap_occ(value, bit):
        return lax.ppermute(value, "occ", [(o, o ^ bit) for o in range(occ_size)])

    def swap_pair(value):
        return lax.ppermute(value, "virt", [(v, v ^ 1) for v in range(virt_size)])

    def shift_ring(value, k):
        return lax.ppermute(value, "virt", [(v, (v - 2 * k) % virt_size) for v in range(virt_size)])

    def mix(value):
        to = [(o ^ 2, v) if o % 2 == 0 else (o, v ^ 1) for o in range(occ_size) for v in range(virt_size)]
        moves = [(n, o * virt_size + v) for n, (o, v) in enumerate(to)]
        return lax.ppermute(value, ("occ", "virt"), moves)

    shifts = sorted(range(1, ring), key=lambda k: min(k, ring - k))
    early, late = shifts[: ring // 2], shifts[ring // 2 :]
    kinds = {"O": [0], "A": early[0::2], "B": early[1::2], "C": late}
    reach = (len(early) + 1) // 2
    plan = {
        ("O", 0, FIRST): ("own", 0, 1),
        ("B", 1, SECOND): ("shift", 4, 4),
        ("A", 0, FIRST): ("ring", 1, 1),
        ("C", 0, SECOND): ("plane", 3, 3),
        ("B", 0, FIRST): ("ring", 2, 2),
        ("B", 1, FIRST): ("shift", 3, 3),
        ("A", 1, SECOND): ("both", 4, 4),
        ("B", 0, SECOND): ("plane", 3, 4),
        ("C", 0, FIRST): ("ring", 2, 2),
        ("C", 1, FIRST): ("pair", 3, 3),
        ("A", 0, SECOND): ("plane", 2, 2),
        ("A", 1, FIRST): ("pair", 2, 2),
        ("C", 1, SECOND): ("both", 4, 4),
        ("O", 0, SECOND): ("own", 1, 1),
        ("O", 1, FIRST): ("pair", 1, 1),
        ("O", 1, SECOND): ("both", 2, 3),
    }
    listed = [((k, side, half), *plan[kind, side, half]) for kind, side, half in plan for k in kinds[kind]]
    stages = 1 + max(group for *_, group in listed)
    groups = [[name for name, _, _, group in listed if group == n] for n in range(stages)]
    places = [[(*name, step) for name in group for step in range(2)] for group in groups]

    where = jnp.stack([virt_index, occ_index]).astype(jnp.int32)
    column = lax.dynamic_slice_in_dim(virt_energy, virt_index * local_virt, local_virt)[:, None]
    virt_halves = virt_energy.reshape(2 * virt_size, half)
    bits = [1 << n for n in range(occ_size.bit_length() - 1)]
    own, sent, held = extract(bits, partners, integrals)
    first, second = choose(held, 0, own, swap_occ(sent, 1))
    rows, row_energy, token, energies = prepare(
        where, partners, occ_energy, column, virt_halves, integrals.reshape(-1, aux_width), [group for group in places if group], first
    )
    sent = [second, first]
    for n, bit in list(enumerate(bits))[1:]:
        (first,) = choose(held, n, first, swap_occ(sent[0] if bit == 2 else first, bit), token)
    for n, bit in list(enumerate(bits))[1:]:
        got = swap_occ(sent[1] if bit == 2 else second, bit)
        (second,) = choose(held, n, second, got, token)

    blocks = {(0, 0, FIRST): first}

    def fetch(name, move):
        k, side, half = name
        if move == "own":
            return second
        if move == "ring":
            near = k - reach if (k - reach, 0, FIRST) in blocks else 0
            return shift_ring(blocks[near, 0, FIRST], k - near)
        if move == "plane":
            return swap_occ(blocks[k, side, FIRST], 2)
        if move == "pair":
            return swap_pair(blocks[k, 0, half])
        if move == "both":
            return mix(pick(blocks[k, 1, FIRST], blocks[k, 0, SECOND]))
        return shift_ring(blocks[0, side, half], k)

    fetched, total = {}, None
    for n in range(stages):
        for name, move, stage, _ in listed:
            if stage == n == 0 and name != (0, 0, FIRST):
                blocks[name] = fetch(name, move)
            if stage == n > 0:
                (blocks[name],) = gate([token], [fetched[name]])
        for name, move, stage, _ in listed:
            if stage == n + 1:
                fetched[name] = fetch(name, move)
        if not groups[n]:
            continue
        pairs = [block for name in groups[n] for block in (blocks[name], swap_occ(blocks[name], 1))]
        waits = [second] if n == 0 else [blocks[name] for name, _, stage, _ in listed if stage == n and name not in groups[n]]
        total, token = contract(rows, row_energy, energies.pop(0), pairs, waits, total, n == stages - 1)
    return total.reshape(integrals.shape)


def solution(mesh):
    in_specs = (P("occ", "virt", None), P(), P(), P())
    out_specs = P("occ", "virt", None)

    def run(integrals, occ_energy, virt_energy, partners):
        return per_device(
            mesh.shape["occ"], mesh.shape["virt"], integrals, occ_energy, virt_energy, partners
        )

    return jax.shard_map(run, mesh=mesh, in_specs=in_specs, out_specs=out_specs, check_vma=False)
```

```python
import jax
import jax.numpy as jnp
from jax import lax
from jax.experimental import pallas as pl
from jax.experimental.pallas import tpu as pltpu
from jax.sharding import PartitionSpec as P

FIRST, SECOND = range(2)

VMEM = pl.BlockSpec(memory_space=pltpu.VMEM)
SMEM = pl.BlockSpec(memory_space=pltpu.SMEM)
ANY = pl.BlockSpec(memory_space=pl.ANY)
TOKEN = jax.ShapeDtypeStruct((8, 128), jnp.float32)


def call(kernel, operands, in_specs, outs, scratch=(), aliases=None, vmem=2):
    return pl.pallas_call(
        kernel,
        in_specs=in_specs,
        out_specs=[spec for spec, _ in outs],
        out_shape=[shape for _, shape in outs],
        scratch_shapes=list(scratch),
        input_output_aliases=aliases or {},
        compiler_params=pltpu.CompilerParams(vmem_limit_bytes=vmem << 20),
        cost_estimate=pl.CostEstimate(flops=0, bytes_accessed=0, transcendentals=0),
    )(*operands)


def padded(depth):
    return depth if depth <= 256 else -(-depth // 256) * 256


def extract(bits, partners, integrals):
    occ_dev = integrals.shape[0]
    shape = pltpu.VMEM(integrals.shape[1:], integrals.dtype)

    def kernel(partners_ref, integrals_ref, own_ref, sent_ref, held_ref, sems):
        occ_index = lax.axis_index("occ")
        core = lax.rem(occ_index, 2)
        copies = []
        for k, (out_ref, step) in enumerate(((sent_ref, 1 - core), (own_ref, core))):
            row = lax.rem(partners_ref[step], occ_dev)
            copies.append(pltpu.make_async_copy(integrals_ref.at[row], out_ref, sems.at[k]))
        for copy in copies:
            copy.start()
        owner = lax.div(partners_ref[core], occ_dev)
        for k, bit in enumerate(bits):
            held = jnp.where(lax.div(owner, bit) == lax.div(occ_index, bit), 1, 0)
            held_ref[pl.ds(8 * k, 8), :] = jnp.full((8, 128), held, jnp.int32)
        for copy in copies:
            copy.wait()

    flags = pltpu.VMEM((8 * len(bits), 128), jnp.int32)
    return call(
        kernel,
        [partners, integrals],
        [SMEM, ANY],
        [(VMEM, shape), (VMEM, shape), (VMEM, flags)],
        [pltpu.SemaphoreType.DMA((2,))],
        vmem=56,
    )


def choose(held, n, own, got, token=None):
    halves = 2 if n == 0 else 1
    depth, width = own.shape[0] // halves, own.shape[1]

    def kernel(held_ref, own_ref, got_ref, *rest):
        out_refs = rest[-halves:]
        plane = lax.rem(lax.div(lax.axis_index("occ"), 2), 2)
        flag = held_ref[8 * n : 8 * n + 1, 0:1] == 1
        for k in range(halves):
            at = pl.multiple_of(lax.rem(plane + k, 2) * depth, depth) if halves == 2 else 0
            rows = pl.ds(at, depth)
            out_refs[k][...] = jnp.where(flag, own_ref[rows, :], got_ref[rows, :])

    operands, specs = [held, own, got], [VMEM] * 3
    if token is not None:
        operands.append(token)
        specs.append(ANY)
    return call(kernel, operands, specs, [(VMEM, pltpu.VMEM((depth, width), own.dtype))] * halves)


def pick(first, second):
    def kernel(first_ref, second_ref, out_ref):
        core = lax.rem(lax.axis_index("occ"), 2)
        flag = jnp.full((1, 1), core, jnp.int32) == 0
        out_ref[...] = jnp.where(flag, first_ref[...], second_ref[...])

    outs = [(VMEM, pltpu.VMEM(first.shape, first.dtype))]
    return call(kernel, [first, second], [VMEM, VMEM], outs)[0]


def prepare(where, partners, occ_energy, virt_halves, rows, groups, ready):
    height = rows.shape[0]
    half = virt_halves.shape[1]
    local_virt = 2 * half
    occ_dev, virt_size = height // local_virt, virt_halves.shape[0] // 2
    widths = [padded(half * len(places)) for places in groups]

    def kernel(where_ref, partners_ref, occ_energy_ref, virt_ref, rows_ref, *rest):
        rest = rest[1:]
        out_ref, row_energy_ref, token_ref = rest[:3]
        energy_refs, sem = rest[3:-1], rest[-1]
        load = pltpu.make_async_copy(rows_ref, out_ref, sem)
        load.start()
        virt_index, occ_index = where_ref[0], where_ref[1]
        plane = lax.rem(lax.div(occ_index, 2), 2)
        token_ref[...] = jnp.zeros_like(token_ref)
        square = [lax.broadcasted_iota(jnp.int32, (half, half), axis) for axis in (0, 1)]
        for part in range(2):
            line = virt_ref[pl.ds(2 * virt_index + part, 1), :]
            column = jnp.sum(jnp.where(square[0] == square[1], line, 0.0), axis=1, keepdims=True)
            for i in range(occ_dev):
                own = occ_energy_ref[occ_index * occ_dev + i]
                row_energy_ref[pl.ds(i * local_virt + part * half, half), :] = column - own
        for places, energy_ref in zip(groups, energy_refs):
            energy_ref[...] = jnp.ones_like(energy_ref)
            for k, (ring_step, side, which, step) in enumerate(places):
                position = lax.rem(virt_index + 2 * ring_step, virt_size)
                position = position + side * (1 - 2 * lax.rem(position, 2))
                pair = occ_energy_ref[partners_ref[lax.rem(occ_index + step, 2)]]
                part = lax.rem(plane + which, 2)
                energy_ref[:, k * half : (k + 1) * half] = virt_ref[pl.ds(2 * position + part, 1), :] - pair
        load.wait()

    outs = [(VMEM, pltpu.VMEM(rows.shape, rows.dtype)), (VMEM, pltpu.VMEM((height, 1), jnp.float32)), (VMEM, TOKEN)]
    outs += [(VMEM, pltpu.VMEM((1, width), jnp.float32)) for width in widths]
    rows, row_energy, token, *energies = call(
        kernel,
        [where, partners, occ_energy, virt_halves, rows, ready],
        [SMEM] * 3 + [VMEM] + [ANY] * 2,
        outs,
        [pltpu.SemaphoreType.DMA],
        vmem=16,
    )
    return rows, row_energy, token, energies


def contract(rows, row_energy, block_energy, blocks, waits, total, last):
    height, width = rows.shape
    count, depths = len(blocks), [block.shape[0] for block in blocks]
    starts, depth = [sum(depths[:k]) for k in range(count)], padded(sum(depths))
    tile = max(t for t in range(16, 513, 16) if height % t == 0)
    tiles = height // tile

    def kernel(rows_ref, row_energy_ref, block_energy_ref, *rest):
        block_refs, rest = rest[:count], rest[count + len(waits) :]
        total_ref, rest = (rest[0], rest[1:]) if total is not None else (None, rest)
        out_ref, token_ref, held, sems = rest[:4]
        copies = [
            pltpu.make_async_copy(block_refs[k], held.at[pl.ds(starts[k], depths[k])], sems.at[k])
            for k in range(count)
        ]
        for copy in copies:
            copy.start()
        token_ref[...] = jnp.zeros_like(token_ref)
        if sum(depths) < depth:
            held[sum(depths) :, :] = jnp.zeros((depth - sum(depths), width), held.dtype)
        for copy in copies:
            copy.wait()
        writes = []
        for i in range(tiles):
            at = pl.ds(i * tile, tile)
            scores = lax.dot_general(
                rows_ref[at, :], held[...], (((1,), (1,)), ((), ())), preferred_element_type=jnp.float32
            )
            amplitudes = (scores / (row_energy_ref[at, :] + block_energy_ref[...])).astype(jnp.bfloat16)
            result = jnp.dot(amplitudes, held[...], preferred_element_type=jnp.float32)
            if total_ref is not None:
                result = result + total_ref[at, :]
            if last:
                staged, write_sems = rest[4:]
                if i >= 2:
                    writes[i - 2].wait()
                staged[i % 2] = result.astype(jnp.bfloat16)
                write = pltpu.make_async_copy(staged.at[i % 2], out_ref.at[at, :], write_sems.at[i])
                write.start()
                writes.append(write)
            else:
                out_ref[at, :] = result
        for write in writes[-2:]:
            write.wait()

    operands = [rows, row_energy, block_energy, *blocks, *waits]
    specs = [VMEM] * 3 + [ANY] * (count + len(waits))
    if total is not None:
        operands.append(total)
        specs.append(VMEM)
    scratch = [pltpu.VMEM((depth, width), jnp.bfloat16), pltpu.SemaphoreType.DMA((count,))]
    if last:
        scratch += [pltpu.VMEM((2, tile, width), jnp.bfloat16), pltpu.SemaphoreType.DMA((tiles,))]
        out = (ANY, jax.ShapeDtypeStruct((height, width), jnp.bfloat16))
    else:
        out = (VMEM, pltpu.VMEM((height, width), jnp.float32))
    aliases = {len(operands) - 1: 0} if total is not None and not last else {}
    return call(kernel, operands, specs, [out, (VMEM, TOKEN)], scratch, aliases, vmem=16)


def gate(tokens, values):
    skip = len(tokens)

    def kernel(*refs):
        del refs

    outs = [(ANY, jax.ShapeDtypeStruct(value.shape, value.dtype)) for value in values]
    aliases = {skip + k: k for k in range(len(values))}
    return call(kernel, [*tokens, *values], [ANY] * (skip + len(values)), outs, aliases=aliases, vmem=1)


def per_device(occ_size, virt_size, integrals, occ_energy, virt_energy, partners):
    occ_dev, local_virt, aux_width = integrals.shape
    occ_index, virt_index = lax.axis_index("occ"), lax.axis_index("virt")
    ring, half = virt_size // 2, local_virt // 2

    def swap_occ(value, bit):
        return lax.ppermute(value, "occ", [(o, o ^ bit) for o in range(occ_size)])

    def swap_pair(value):
        return lax.ppermute(value, "virt", [(v, v ^ 1) for v in range(virt_size)])

    def shift_ring(value, k):
        return lax.ppermute(value, "virt", [(v, (v - 2 * k) % virt_size) for v in range(virt_size)])

    def mix(value):
        to = [(o ^ 2, v) if o % 2 == 0 else (o, v ^ 1) for o in range(occ_size) for v in range(virt_size)]
        moves = [(n, o * virt_size + v) for n, (o, v) in enumerate(to)]
        return lax.ppermute(value, ("occ", "virt"), moves)

    shifts = sorted(range(1, ring), key=lambda k: min(k, ring - k))
    early, late = shifts[: ring // 2], shifts[ring // 2 :]
    kinds = {"O": [0], "A": early[0::2], "B": early[1::2], "C": late}
    reach = (len(early) + 1) // 2
    plan = {
        ("O", 0, FIRST): ("own", 0, 1),
        ("B", 1, SECOND): ("shift", 4, 4),
        ("A", 0, FIRST): ("ring", 1, 1),
        ("C", 0, SECOND): ("plane", 3, 3),
        ("B", 0, FIRST): ("ring", 2, 2),
        ("B", 1, FIRST): ("shift", 3, 3),
        ("A", 1, SECOND): ("both", 4, 4),
        ("B", 0, SECOND): ("plane", 3, 4),
        ("C", 0, FIRST): ("ring", 2, 2),
        ("C", 1, FIRST): ("pair", 3, 3),
        ("A", 0, SECOND): ("plane", 2, 2),
        ("A", 1, FIRST): ("pair", 2, 2),
        ("C", 1, SECOND): ("both", 4, 4),
        ("O", 0, SECOND): ("own", 1, 1),
        ("O", 1, FIRST): ("pair", 1, 1),
        ("O", 1, SECOND): ("both", 2, 3),
    }
    listed = [((k, side, half), *plan[kind, side, half]) for kind, side, half in plan for k in kinds[kind]]
    stages = 1 + max(group for *_, group in listed)
    groups = [[name for name, _, _, group in listed if group == n] for n in range(stages)]
    places = [[(*name, step) for name in group for step in range(2)] for group in groups]

    where = jnp.stack([virt_index, occ_index]).astype(jnp.int32)
    virt_halves = virt_energy.reshape(2 * virt_size, half)
    bits = [1 << n for n in range(occ_size.bit_length() - 1)]
    own, sent, held = extract(bits, partners, integrals)
    first, second = choose(held, 0, own, swap_occ(sent, 1))
    rows, row_energy, token, energies = prepare(
        where, partners, occ_energy, virt_halves, integrals.reshape(-1, aux_width), [group for group in places if group], first
    )
    sent = [second, first]
    for n, bit in list(enumerate(bits))[1:]:
        (first,) = choose(held, n, first, swap_occ(sent[0] if bit == 2 else first, bit), token)
    for n, bit in list(enumerate(bits))[1:]:
        got = swap_occ(sent[1] if bit == 2 else second, bit)
        (second,) = choose(held, n, second, got, token)

    blocks = {(0, 0, FIRST): first}

    def fetch(name, move):
        k, side, half = name
        if move == "own":
            return second
        if move == "ring":
            near = k - reach if (k - reach, 0, FIRST) in blocks else 0
            return shift_ring(blocks[near, 0, FIRST], k - near)
        if move == "plane":
            return swap_occ(blocks[k, side, FIRST], 2)
        if move == "pair":
            return swap_pair(blocks[k, 0, half])
        if move == "both":
            return mix(pick(blocks[k, 1, FIRST], blocks[k, 0, SECOND]))
        return shift_ring(blocks[0, side, half], k)

    fetched, total = {}, None
    for n in range(stages):
        for name, move, stage, _ in listed:
            if stage == n == 0 and name != (0, 0, FIRST):
                blocks[name] = fetch(name, move)
            if stage == n > 0:
                (blocks[name],) = gate([token], [fetched[name]])
        for name, move, stage, _ in listed:
            if stage == n + 1:
                fetched[name] = fetch(name, move)
        if not groups[n]:
            continue
        pairs = [block for name in groups[n] for block in (blocks[name], swap_occ(blocks[name], 1))]
        waits = [second] if n == 0 else [blocks[name] for name, _, stage, _ in listed if stage == n and name not in groups[n]]
        total, token = contract(rows, row_energy, energies.pop(0), pairs, waits, total, n == stages - 1)
    return total.reshape(integrals.shape)


def solution(mesh):
    in_specs = (P("occ", "virt", None), P(), P(), P())
    out_specs = P("occ", "virt", None)

    def run(integrals, occ_energy, virt_energy, partners):
        return per_device(
            mesh.shape["occ"], mesh.shape["virt"], integrals, occ_energy, virt_energy, partners
        )

    return jax.shard_map(run, mesh=mesh, in_specs=in_specs, out_specs=out_specs, check_vma=False)
```
